32 devices in a mesh: groups: 2 (over y), row: 16 (over z, x, core).
Axes of the slice: x: 2, y: 2, z: 4, core: 2. Of those that a mesh axis runs over, the one named last changes fastest.
Arguments:
- spectra: bfloat16 [2, 2, 8192, 8192], P('groups', None, None, 'row'), parts along dimension 0, may hold values from -1.5 to 1.5
- pattern: int32 [64, 64], replicated, may hold values from 0 to 1, as said below
- counts: int32 [8192], replicated, may hold values from 1 to 8
Outputs:
- multiples: bfloat16 [2, 2, 8192, 8192], P('groups', None, 'row'), parts along dimension 0
The draws below stay inside these ranges and needn't reach their ends.
There are 2 independent parts, one for each index of `groups`. The reference program is written for one: setup_inputs(seed, part) draws one part's arguments, and reference() takes and returns one part's arrays. A program takes and returns all parts, laid end to end along the dimension named above; an argument that names none is the same for every part. Nothing has to cross between parts.
Inputs may be any that keep to these rules, and one draw needn't show every extreme that they name: pattern[I, K] is 0 or 1, is 0 wherever |I - K| > 2, and is 1 on the diagonal.
All inputs are finite; a program needn't handle non-finite values.
Results may differ from the reference program's by a relative error of at most 0.0025.
Values may be sent and summed in bfloat16 or wider, within the bound.
A program may use at most 256 MiB of HBM per device.

```python
import jax
import jax.numpy as jnp
from jax import lax

N = 8192
TILE = 128
REACH = 2
FREQS = 1
NT = 64


def draw_pattern(key, part):
    key = jax.random.fold_in(key, 11)
    tiles = N // TILE
    coin = jax.random.randint(key, (tiles, tiles), 0, 5)
    across = jnp.arange(tiles, dtype=jnp.int32)[:, None]
    along = jnp.arange(tiles, dtype=jnp.int32)[None, :]
    inside = jnp.abs(across - along) <= REACH
    kept = jnp.where(across == along, 1, jnp.where(inside & (coin < 3), 1, 0))
    return kept.astype(jnp.int32)


def touch_ends(drawn, rng, least, high):
    extent = drawn.shape
    spot = [jax.random.randint(jax.random.fold_in(rng, axis), (), 0, extent[axis]) for axis in range(len(extent))]
    drawn = drawn.at[tuple(spot)].set(least)
    longest = extent.index(max(extent))
    spot[longest] = (spot[longest] + 1) % extent[longest]
    return drawn.at[tuple(spot)].set(high)


def block_levels(stream_key, shape, shards, smallest, high):
    gain, own = 1.0, jax.random.fold_in(stream_key, 6)
    for dim, blocks in shards:
        heights = jnp.exp(jax.random.uniform(jax.random.fold_in(own, dim), (blocks,), jnp.float32, smallest / len(shards), high / len(shards)))
        gain = gain * jnp.repeat(heights, shape[dim] // blocks).reshape([-1 if axis == dim else 1 for axis in range(len(shape))])
    return gain


def scatter_about(stream_key, shape, deviation, bound, shards=(), held_as=jnp.bfloat16):
    values = deviation * jax.random.normal(stream_key, shape, jnp.float32)
    if shards:
        values = values * block_levels(stream_key, shape, shards, -0.22, 0.18)
    return jnp.clip(values, -bound, bound).astype(held_as)


def setup_inputs(seed: int = 0, part: int = 0) -> dict:
    key_list = jax.random.split(jax.random.key(seed), 4)
    own_keys = jax.random.split(jax.random.fold_in(key_list[3], part), 4)
    return {
        "spectra": scatter_about(own_keys[0], (FREQS, 2, N, N), 0.25, 1.5, ((3, 16),)),
        "pattern": draw_pattern(jax.random.fold_in(key_list[3], 71), part),
        "counts": touch_ends(jax.random.randint(key_list[2], (N,), 1, 9), jax.random.fold_in(key_list[2], 1), 1, 8).astype(jnp.int32),
    }


def reference(spectra, pattern, counts):
    weights = 1.0 / counts.astype(jnp.float32)
    span = (2 * REACH + 1) * TILE
    margin = REACH * TILE
    zero_index = jnp.zeros((), jnp.int32)
    margin_index = jnp.full((), margin, jnp.int32)
    pattern_padded = jnp.pad(pattern.astype(jnp.float32), ((0, 0), (REACH, REACH)))
    weights_padded = jnp.pad(weights, (margin, margin))
    results = []
    for number in range(FREQS):
        field = jnp.pad(spectra[number], ((0, 0), (margin, margin), (margin, margin)))

        def tile_rows(tile):
            tile = tile.astype(jnp.int32)
            start = (tile * TILE).astype(jnp.int32)
            left = lax.dynamic_slice(field, (zero_index, (start + margin_index).astype(jnp.int32), start), (2, TILE, span))
            right = lax.dynamic_slice(field, (zero_index, start, margin_index), (2, span, N))
            tile_mask = lax.dynamic_slice(pattern_padded, (tile, tile), (1, 2 * REACH + 1))[0]
            factor = jnp.repeat(tile_mask, TILE) * lax.dynamic_slice(weights_padded, (start,), (span,))
            left = (left.astype(jnp.float32) * factor[None, None, :]).astype(jnp.bfloat16)
            stacked = jnp.concatenate([jnp.concatenate([left[0], -left[1]], axis=1),
                                       jnp.concatenate([left[1], left[0]], axis=1)], axis=0)
            product = jnp.dot(stacked, right.reshape(2 * span, N), preferred_element_type=jnp.float32)
            return product.astype(jnp.bfloat16).reshape(2, TILE, N)

        blocks = lax.map(tile_rows, jnp.arange(NT, dtype=jnp.int32))
        results.append(jnp.transpose(blocks, (1, 0, 2, 3)).reshape(2, N, N))
    return jnp.stack(results)
```

```python
import functools

import jax
import jax.numpy as jnp
from jax import lax
from jax.experimental import pallas as pl
from jax.experimental.pallas import tpu as pltpu
from jax.sharding import PartitionSpec as P

TILE = 128
REACH = 2
WIDE = 2 * REACH + 1
CORES = 4
AHEAD = 2
VMEM_BYTES = 62 * 2**20


def from_behind(value, axis, steps):
    count = lax.axis_size(axis)
    initial, last = (max(0, -steps), min(count, count - steps))
    return lax.ppermute(value, axis, [(source, source + steps) for source in range(initial, last)])


def by_rows(spectra, pattern, counts):
    total = spectra.shape[2]
    rows_dev = spectra.shape[3]
    place = lax.axis_index("row")
    margin = REACH * TILE
    span = max(rows_dev, TILE) + 2 * margin
    tiles = total // TILE
    first_tile = place * rows_dev // TILE
    offset_rows = place * rows_dev - first_tile * TILE
    own_rows = lax.all_to_all(spectra, "row", split_axis=2, concat_axis=3, tiled=True)
    below = (margin + max(TILE - rows_dev, 0) + rows_dev - 1) // rows_dev
    above = (span - margin + rows_dev - 1) // rows_dev - 1
    pieces = []
    for offset in range(-below, above + 1):
        if offset == 0:
            pieces.append(own_rows)
        else:
            pieces.append(from_behind(own_rows, "row", -offset))
    joined = jnp.concatenate(pieces, axis=2)
    window = lax.dynamic_slice_in_dim(joined, below * rows_dev - margin - offset_rows, span, 2)
    tile_range = jnp.arange(tiles, dtype=jnp.int32)
    row_ids = place * rows_dev + jnp.arange(rows_dev, dtype=jnp.int32)
    inner_ids = (first_tile - REACH) * TILE + jnp.arange(span, dtype=jnp.int32)
    row_onehot = (row_ids[:, None] // TILE == tile_range[None, :]).astype(jnp.float32)
    inner_onehot = (inner_ids[:, None] // TILE == tile_range[None, :]).astype(jnp.float32)
    pattern_rows = jnp.dot(row_onehot, pattern.astype(jnp.float32), precision=lax.Precision.HIGHEST)
    aperture = jnp.dot(pattern_rows, inner_onehot.T, precision=lax.Precision.HIGHEST)
    padded_counts = jnp.pad(counts, (margin, margin), constant_values=1)
    weights = 1.0 / lax.dynamic_slice_in_dim(padded_counts, first_tile * TILE, span).astype(
        jnp.float32
    )
    factor = aperture * weights[None, :]
    wide_rows = jnp.pad(own_rows, ((0, 0), (0, 0), (0, 0), (margin, margin)))
    columns = lax.dynamic_slice_in_dim(wide_rows, first_tile * TILE, span, 3)
    left = (columns[0].astype(jnp.float32) * factor[None]).astype(jnp.bfloat16)
    stacked_left = jnp.concatenate(
        [jnp.concatenate([left[0], -left[1]], axis=1), jnp.concatenate([left[1], left[0]], axis=1)],
        axis=0,
    )
    product = jnp.dot(
        stacked_left, window[0].reshape(2 * span, total), preferred_element_type=jnp.float32
    )
    results = [product.astype(jnp.bfloat16).reshape(2, rows_dev, total)]
    return jnp.stack(results)


def window_start(tile, tiles):
    return jnp.clip(tile - REACH, 0, tiles - WIDE)


def plane_kernel(planes, src, pat, weights, out, held, band, left, done,
                 band_send, band_recv, edge_send, edge_recv,
                 part_send, part_recv, out_send, out_recv):
    tiles = src.shape[1]
    cols = src.shape[3]
    own_tiles = cols // TILE
    plane_tiles = CORES * own_tiles
    me = lax.axis_index("row")
    plane = me // CORES
    m = me % CORES
    core_mate = me + 1 - 2 * (me % 2)
    x_mate = plane * CORES + (m + 2) % CORES
    first = plane * plane_tiles
    low_first = m >= 2

    def device(index):
        return dict(device_id={"row": index}, device_id_type=pl.DeviceIdType.MESH)

    barrier = pltpu.get_barrier_semaphore()
    count = planes * CORES

    def greet(step, carry):
        pl.semaphore_signal(barrier, inc=1, **device(lax.rem(me + step, count)))
        return carry

    lax.fori_loop(1, count, greet, 0)
    pl.semaphore_wait(barrier, count - 1)

    def band_view(u):
        tile = me * own_tiles + u
        return src.at[:, pl.ds(window_start(tile, tiles), WIDE), :, pl.ds(u * TILE, TILE)]

    def band_slot(member, u):
        return band.at[member * own_tiles + u + REACH]

    def band_copy(kind, member, u, target):
        source = band_slot(member, u) if kind == 2 else band_view(u)
        return pltpu.make_async_remote_copy(
            src_ref=source, dst_ref=band_slot(member, u),
            send_sem=band_send.at[kind, u], recv_sem=band_recv.at[kind, u], **device(target))

    def band_local(u):
        return pltpu.make_async_copy(band_view(u), band_slot(m, u), band_recv.at[3, u])

    for u in range(own_tiles):
        band_copy(1, m, u, x_mate).start()
    for u in range(own_tiles):
        band_local(u).start()
        band_copy(0, m, u, core_mate).start()

    def edge_copy(side, u, dest):
        if side == 0:
            column = own_tiles - REACH + u
            row, slot, place = me * own_tiles + column + 1, u, WIDE - REACH
        else:
            column = u
            row, slot, place = me * own_tiles + column - REACH, plane_tiles + REACH + u, 0
        row = jnp.clip(row, 0, tiles - REACH)
        return pltpu.make_async_remote_copy(
            src_ref=src.at[:, pl.ds(row, REACH), :, pl.ds(column * TILE, TILE)],
            dst_ref=band.at[slot, :, pl.ds(place, REACH)],
            send_sem=edge_send.at[side, u, dest % CORES], recv_sem=edge_recv.at[side, u],
            **device(dest))

    sends_low = jnp.logical_and(m == CORES - 1, plane < planes - 1)
    sends_high = jnp.logical_and(m == 0, plane > 0)

    @pl.when(sends_low)
    def _():
        for u in range(REACH):
            for mate in range(CORES):
                edge_copy(0, u, (plane + 1) * CORES + mate).start()

    @pl.when(sends_high)
    def _():
        for u in range(REACH):
            for mate in range(CORES):
                edge_copy(1, u, (plane - 1) * CORES + mate).start()

    def parts(step, to_plane, from_plane, act, local=False):
        base = to_plane * plane_tiles

        def piece(start, size, c, slot):
            source = src.at[c, pl.ds(base - REACH + start, size)]
            dest = held.at[from_plane, pl.ds(start, size), c]
            if local:
                return pltpu.make_async_copy(source, dest, part_recv.at[from_plane, slot, c])
            return pltpu.make_async_remote_copy(
                src_ref=source, dst_ref=dest,
                send_sem=part_send.at[to_plane, slot, c],
                recv_sem=part_recv.at[from_plane, slot, c],
                **device(to_plane * CORES + m))

        slot = jnp.where(low_first, step, CORES + 1 - step)

        def both(start, size):
            for c in range(2):
                act(piece(start, size, c, slot))

        if 1 <= step <= CORES:
            both(REACH + (slot - 1) * own_tiles, own_tiles)
        else:
            @pl.when(jnp.logical_and(slot == 0, to_plane > 0))
            def _():
                both(0, REACH)

            @pl.when(jnp.logical_and(slot == CORES + 1, to_plane < planes - 1))
            def _():
                both(REACH + plane_tiles, REACH)

    def start(copy):
        copy.start()

    steps = CORES + 2
    offsets = [o for k in range(1, planes // 2 + 1) for o in dict.fromkeys((k, planes - k))]

    def send_step(step):
        for o in offsets:
            parts(step, lax.rem(plane + o, planes), plane, start)

    for step in range(steps):
        parts(step, plane, plane, start, local=True)
    for step in range(AHEAD):
        send_step(step)

    for u in range(own_tiles):
        band_copy(1, (m + 2) % CORES, u, x_mate).wait_recv()
        band_copy(2, (m + 2) % CORES, u, core_mate).start()
    core_m = core_mate % CORES
    for u in range(own_tiles):
        band_local(u).wait()
        band_copy(0, core_m, u, core_mate).wait_recv()
        band_copy(2, (core_m + 2) % CORES, u, core_mate).wait_recv()

    @pl.when(plane > 0)
    def _():
        for u in range(REACH):
            edge_copy(0, u, me).wait_recv()

    @pl.when(plane < planes - 1)
    def _():
        for u in range(REACH):
            edge_copy(1, u, me).wait_recv()

    def build(index, carry):
        i, t = index // WIDE, index % WIDE
        tile = first + i
        inner = window_start(tile, tiles) + t
        j = jnp.clip(tile - window_start(inner, tiles), 0, WIDE - 1)
        slot = inner - first + REACH
        factor = pat[tile, inner].astype(jnp.float32) * weights[pl.ds(inner, 1), :]
        re = (band[slot, 0, j].astype(jnp.float32) * factor).astype(jnp.bfloat16)
        im = (band[slot, 1, j].astype(jnp.float32) * factor).astype(jnp.bfloat16)
        left[i, t, 0:TILE, 0:TILE] = re
        left[i, t, 0:TILE, TILE:2 * TILE] = -im
        left[i, t, TILE:2 * TILE, 0:TILE] = im
        left[i, t, TILE:2 * TILE, TILE:2 * TILE] = re
        return carry

    lax.fori_loop(0, plane_tiles * WIDE, build, 0)

    def out_copy(from_plane, group, sender, local=False):
        dest = out.at[:, :, pl.ds(pl.multiple_of((from_plane * CORES + sender) * cols, cols), cols)]
        source = done.at[from_plane, group]
        if local:
            return pltpu.make_async_copy(source, dest, out_send.at[from_plane, group])
        return pltpu.make_async_remote_copy(
            src_ref=source, dst_ref=dest,
            send_sem=out_send.at[from_plane, group], recv_sem=out_recv.at[from_plane, sender],
            **device(plane * CORES + group))

    def multiply(order, from_plane):
        group = jnp.where(low_first, order, CORES - 1 - order)

        def one(r, carry):
            i = group * own_tiles + r
            begin = window_start(first + i, tiles) - first + REACH
            total = None
            for t in range(WIDE):
                term = jnp.dot(left[i, t], held[from_plane, begin + t].reshape(2 * TILE, cols),
                               preferred_element_type=jnp.float32)
                total = term if total is None else total + term
            rows = pl.ds(pl.multiple_of(r * TILE, TILE), TILE)
            done[from_plane, group, 0, rows, :] = total[:TILE].astype(jnp.bfloat16)
            done[from_plane, group, 1, rows, :] = total[TILE:].astype(jnp.bfloat16)
            return carry

        lax.fori_loop(0, own_tiles, one, 0)

        @pl.when(group == m)
        def _():
            out_copy(from_plane, group, m, local=True).start()

        @pl.when(group != m)
        def _():
            out_copy(from_plane, group, m).start()

    for step in range(steps):
        parts(step, plane, plane, lambda copy: copy.wait(), local=True)

    def own(order, carry):
        multiply(order, plane)
        return carry

    lax.fori_loop(0, CORES, own, 0)

    for step in range(steps):
        if step and step + AHEAD - 1 < steps:
            send_step(step + AHEAD - 1)
        for o in offsets:
            sender = lax.rem(plane + planes - o, planes)
            parts(step, plane, sender, lambda copy: copy.wait_recv())
            if step >= 2:
                multiply(step - 2, sender)

    for u in range(own_tiles):
        for kind in range(3):
            band_copy(kind, m, u, core_mate).wait_send()

    @pl.when(sends_low)
    def _():
        for u in range(REACH):
            for mate in range(CORES):
                edge_copy(0, u, (plane + 1) * CORES + mate).wait_send()

    @pl.when(sends_high)
    def _():
        for u in range(REACH):
            for mate in range(CORES):
                edge_copy(1, u, (plane - 1) * CORES + mate).wait_send()

    for step in range(steps):
        for o in offsets:
            parts(step, lax.rem(plane + o, planes), plane, lambda copy: copy.wait_send())

    def finish(index, carry):
        from_plane, group = index // CORES, index % CORES

        @pl.when(group == m)
        def _():
            out_copy(from_plane, group, m, local=True).wait()

        @pl.when(group != m)
        def _():
            out_copy(from_plane, group, m).wait_send()
            out_copy(from_plane, group, group).wait_recv()

        return carry

    lax.fori_loop(0, planes * CORES, finish, 0)


def by_planes(spectra, pattern, counts):
    _, parts, total, cols = spectra.shape
    devices = lax.axis_size("row")
    planes = devices // CORES
    tiles = total // TILE
    own_tiles = cols // TILE
    plane_tiles = CORES * own_tiles
    reach_tiles = plane_tiles + 2 * REACH
    weights = (1.0 / counts.astype(jnp.float32)).reshape(tiles, TILE)
    dma = pltpu.SemaphoreType.DMA
    product = pl.pallas_call(
        functools.partial(plane_kernel, planes),
        out_shape=jax.ShapeDtypeStruct((parts, cols, total), jnp.bfloat16),
        in_specs=[
            pl.BlockSpec(memory_space=pl.ANY),
            pl.BlockSpec(memory_space=pltpu.SMEM),
            pl.BlockSpec(memory_space=pltpu.VMEM),
        ],
        out_specs=pl.BlockSpec(memory_space=pl.ANY),
        scratch_shapes=[
            pltpu.VMEM((planes, reach_tiles, 2, TILE, cols), jnp.bfloat16),
            pltpu.VMEM((reach_tiles, 2, WIDE, TILE, TILE), jnp.bfloat16),
            pltpu.VMEM((plane_tiles, WIDE, 2 * TILE, 2 * TILE), jnp.bfloat16),
            pltpu.VMEM((planes, CORES, 2, cols, cols), jnp.bfloat16),
            dma((3, own_tiles)),
            dma((4, own_tiles)),
            dma((2, REACH, CORES)),
            dma((2, REACH)),
            dma((planes, CORES + 2, 2)),
            dma((planes, CORES + 2, 2)),
            dma((planes, CORES)),
            dma((planes, CORES)),
        ],
        compiler_params=pltpu.CompilerParams(
            collective_id=0, has_side_effects=True, vmem_limit_bytes=VMEM_BYTES),
        cost_estimate=pl.CostEstimate(
            flops=4 * total * parts * cols * WIDE * TILE, bytes_accessed=2 * spectra.nbytes, transcendentals=0),
    )(spectra.reshape(parts, tiles, TILE, cols), pattern, weights)
    return product[None]


def fits(spectra):
    devices = lax.axis_size("row")
    cols = spectra.shape[3]
    return devices % CORES == 0 and devices > CORES and cols % (2 * TILE) == 0 and spectra.shape[0] == 1


def per_device(spectra, pattern, counts):
    if fits(spectra):
        return by_planes(spectra, pattern, counts)
    return by_rows(spectra, pattern, counts)


def solution(mesh):
    return jax.shard_map(
        per_device,
        mesh=mesh,
        in_specs=(P("groups", None, None, "row"), P(), P()),
        out_specs=P("groups", None, "row", None),
        check_vma=False,
    )
```

```python
import functools

import jax
import jax.numpy as jnp
from jax import lax
from jax.experimental import pallas as pl
from jax.experimental.pallas import tpu as pltpu
from jax.sharding import PartitionSpec as P

TILE = 128
REACH = 2
WIDE = 2 * REACH + 1
CORES = 4
AHEAD = 4
VMEM_BYTES = 62 * 2**20


def from_behind(value, axis, steps):
    count = lax.axis_size(axis)
    initial, last = (max(0, -steps), min(count, count - steps))
    return lax.ppermute(value, axis, [(source, source + steps) for source in range(initial, last)])


def by_rows(spectra, pattern, counts):
    total = spectra.shape[2]
    rows_dev = spectra.shape[3]
    place = lax.axis_index("row")
    margin = REACH * TILE
    span = max(rows_dev, TILE) + 2 * margin
    tiles = total // TILE
    first_tile = place * rows_dev // TILE
    offset_rows = place * rows_dev - first_tile * TILE
    own_rows = lax.all_to_all(spectra, "row", split_axis=2, concat_axis=3, tiled=True)
    below = (margin + max(TILE - rows_dev, 0) + rows_dev - 1) // rows_dev
    above = (span - margin + rows_dev - 1) // rows_dev - 1
    pieces = []
    for offset in range(-below, above + 1):
        if offset == 0:
            pieces.append(own_rows)
        else:
            pieces.append(from_behind(own_rows, "row", -offset))
    joined = jnp.concatenate(pieces, axis=2)
    window = lax.dynamic_slice_in_dim(joined, below * rows_dev - margin - offset_rows, span, 2)
    tile_range = jnp.arange(tiles, dtype=jnp.int32)
    row_ids = place * rows_dev + jnp.arange(rows_dev, dtype=jnp.int32)
    inner_ids = (first_tile - REACH) * TILE + jnp.arange(span, dtype=jnp.int32)
    row_onehot = (row_ids[:, None] // TILE == tile_range[None, :]).astype(jnp.float32)
    inner_onehot = (inner_ids[:, None] // TILE == tile_range[None, :]).astype(jnp.float32)
    pattern_rows = jnp.dot(row_onehot, pattern.astype(jnp.float32), precision=lax.Precision.HIGHEST)
    aperture = jnp.dot(pattern_rows, inner_onehot.T, precision=lax.Precision.HIGHEST)
    padded_counts = jnp.pad(counts, (margin, margin), constant_values=1)
    weights = 1.0 / lax.dynamic_slice_in_dim(padded_counts, first_tile * TILE, span).astype(
        jnp.float32
    )
    factor = aperture * weights[None, :]
    wide_rows = jnp.pad(own_rows, ((0, 0), (0, 0), (0, 0), (margin, margin)))
    columns = lax.dynamic_slice_in_dim(wide_rows, first_tile * TILE, span, 3)
    left = (columns[0].astype(jnp.float32) * factor[None]).astype(jnp.bfloat16)
    stacked_left = jnp.concatenate(
        [jnp.concatenate([left[0], -left[1]], axis=1), jnp.concatenate([left[1], left[0]], axis=1)],
        axis=0,
    )
    product = jnp.dot(
        stacked_left, window[0].reshape(2 * span, total), preferred_element_type=jnp.float32
    )
    results = [product.astype(jnp.bfloat16).reshape(2, rows_dev, total)]
    return jnp.stack(results)


def window_start(tile, tiles):
    return jnp.clip(tile - REACH, 0, tiles - WIDE)


def plane_kernel(planes, src, pat, weights, out, held, band, left, done,
                 band_send, band_recv, edge_send, edge_recv,
                 part_send, part_recv, pass_send, out_send, out_recv):
    tiles = src.shape[1]
    cols = src.shape[3]
    own_tiles = cols // TILE
    plane_tiles = CORES * own_tiles
    me = lax.axis_index("row")
    plane = me // CORES
    m = me % CORES
    core_mate = me + 1 - 2 * (me % 2)
    x_mate = plane * CORES + (m + 2) % CORES
    first = plane * plane_tiles
    low_first = m >= 2
    odd = plane % 2
    far_planes = [2 - 2 * (plane // 2) + k for k in range(2)]

    def device(index):
        return dict(device_id={"row": index}, device_id_type=pl.DeviceIdType.MESH)

    barrier = pltpu.get_barrier_semaphore()
    count = planes * CORES

    def greet(step, carry):
        pl.semaphore_signal(barrier, inc=1, **device(lax.rem(me + step, count)))
        return carry

    lax.fori_loop(1, count, greet, 0)
    pl.semaphore_wait(barrier, count - 1)

    def band_view(u):
        tile = me * own_tiles + u
        return src.at[:, pl.ds(window_start(tile, tiles), WIDE), :, pl.ds(u * TILE, TILE)]

    def band_slot(member, u):
        return band.at[member * own_tiles + u + REACH]

    def band_copy(kind, member, u, target):
        source = band_slot(member, u) if kind == 2 else band_view(u)
        return pltpu.make_async_remote_copy(
            src_ref=source, dst_ref=band_slot(member, u),
            send_sem=band_send.at[kind, u], recv_sem=band_recv.at[kind, u], **device(target))

    def band_local(u):
        return pltpu.make_async_copy(band_view(u), band_slot(m, u), band_recv.at[3, u])

    for u in range(own_tiles):
        band_copy(1, m, u, x_mate).start()
    for u in range(own_tiles):
        band_local(u).start()
        band_copy(0, m, u, core_mate).start()

    def edge_copy(side, u, dest, relay=0):
        if side == 0:
            column = own_tiles - REACH + u
            row, slot, place = me * own_tiles + column + 1, u, WIDE - REACH
        else:
            column = u
            row, slot, place = me * own_tiles + column - REACH, plane_tiles + REACH + u, 0
        row = jnp.clip(row, 0, tiles - REACH)
        landing = band.at[slot, :, pl.ds(place, REACH)]
        source = landing if relay else src.at[:, pl.ds(row, REACH), :, pl.ds(column * TILE, TILE)]
        return pltpu.make_async_remote_copy(
            src_ref=source, dst_ref=landing,
            send_sem=edge_send.at[side, u, relay], recv_sem=edge_recv.at[side, u],
            **device(dest))

    sends_low = jnp.logical_and(m == CORES - 1, plane < planes - 1)
    sends_high = jnp.logical_and(m == 0, plane > 0)

    @pl.when(sends_low)
    def _():
        for u in range(REACH):
            edge_copy(0, u, (plane + 1) * CORES + m).start()

    @pl.when(sends_high)
    def _():
        for u in range(REACH):
            edge_copy(1, u, (plane - 1) * CORES + m).start()

    units = plane_tiles // REACH + 2

    def unit_copy(unit, to_plane, from_plane):
        start = unit * REACH
        return pltpu.make_async_remote_copy(
            src_ref=src.at[:, pl.ds(to_plane * plane_tiles - REACH + start, REACH)],
            dst_ref=held.at[from_plane, :, pl.ds(start, REACH)],
            send_sem=part_send.at[to_plane, unit], recv_sem=part_recv.at[from_plane, unit],
            **device(to_plane * CORES + m))

    def parts(step, to_plane, from_plane, receiving, act):
        low_edge = to_plane % 2 == 1
        shared = jnp.where(low_edge, 1, units - 2)
        far = to_plane // 2 != from_plane // 2

        def one_end(unit):
            exists = jnp.where(unit == 0, to_plane > 0, to_plane < planes - 1)
            passed_on = jnp.logical_and(far, jnp.where(low_edge, unit == 0, unit == units - 1))
            if not receiving:
                exists = jnp.logical_and(exists, jnp.logical_not(passed_on))

            @pl.when(exists)
            def _():
                act(unit_copy(unit, to_plane, from_plane))

        if step == 0:
            act(unit_copy(shared, to_plane, from_plane))
        elif step == 1:
            one_end(jnp.where(low_first, 0, units - 1))
        elif step == units - 1:
            one_end(jnp.where(low_first, units - 1, 0))
        else:
            j = step - 2
            act(unit_copy(jnp.where(low_first, jnp.where(low_edge, 2 + j, 1 + j),
                                    jnp.where(low_edge, units - 2 - j, units - 3 - j)),
                          to_plane, from_plane))

    def pass_on(from_plane, act):
        mine = jnp.where(odd == 1, 1, units - 2)
        theirs = jnp.where(odd == 1, units - 1, 0)
        act(pltpu.make_async_remote_copy(
            src_ref=held.at[from_plane, :, pl.ds(mine * REACH, REACH)],
            dst_ref=held.at[from_plane, :, pl.ds(theirs * REACH, REACH)],
            send_sem=pass_send.at[from_plane], recv_sem=part_recv.at[from_plane, theirs],
            **device((plane + 1 - 2 * odd) * CORES + m)))

    def own_columns(act):
        def piece(start, size, k):
            act(pltpu.make_async_copy(
                src.at[:, pl.ds(first - REACH + start, size)],
                held.at[plane, :, pl.ds(start, size)], part_recv.at[plane, k]))

        piece(REACH, plane_tiles, 1)

        @pl.when(plane > 0)
        def _():
            piece(0, REACH, 0)

        @pl.when(plane < planes - 1)
        def _():
            piece(REACH + plane_tiles, REACH, units - 1)

    def start(copy):
        copy.start()

    steps = units
    offsets = [o for k in range(1, planes // 2 + 1) for o in dict.fromkeys((k, planes - k))]

    def send_step(step):
        for o in offsets:
            parts(step, lax.rem(plane + o, planes), plane, False, start)

    own_columns(start)
    for step in range(AHEAD):
        send_step(step)

    for u in range(own_tiles):
        band_copy(1, (m + 2) % CORES, u, x_mate).wait_recv()
        band_copy(2, (m + 2) % CORES, u, core_mate).start()
    core_m = core_mate % CORES
    for u in range(own_tiles):
        band_local(u).wait()
        band_copy(0, core_m, u, core_mate).wait_recv()
        band_copy(2, (core_m + 2) % CORES, u, core_mate).wait_recv()

    relays_low = jnp.logical_and(m == CORES - 1, plane > 0)
    relays_high = jnp.logical_and(m == 0, plane < planes - 1)

    def edge_relay(side, act):
        for u in range(REACH):
            for hop in range(1, CORES):
                act(edge_copy(side, u, plane * CORES + (m + hop) % CORES, hop))

    for side, present, relays in ((0, plane > 0, relays_low), (1, plane < planes - 1, relays_high)):
        @pl.when(present)
        def _(side=side):
            for u in range(REACH):
                edge_copy(side, u, me).wait_recv()

        @pl.when(relays)
        def _(side=side):
            edge_relay(side, lambda copy: copy.start())

    def build(index, carry):
        i, t = index // WIDE, index % WIDE
        tile = first + i
        inner = window_start(tile, tiles) + t
        j = jnp.clip(tile - window_start(inner, tiles), 0, WIDE - 1)
        slot = inner - first + REACH
        factor = pat[tile, inner].astype(jnp.float32) * weights[pl.ds(inner, 1), :]
        re = (band[slot, 0, j].astype(jnp.float32) * factor).astype(jnp.bfloat16)
        im = (band[slot, 1, j].astype(jnp.float32) * factor).astype(jnp.bfloat16)
        left[i, t, 0:TILE, 0:TILE] = re
        left[i, t, 0:TILE, TILE:2 * TILE] = -im
        left[i, t, TILE:2 * TILE, 0:TILE] = im
        left[i, t, TILE:2 * TILE, TILE:2 * TILE] = re
        return carry

    lax.fori_loop(0, plane_tiles * WIDE, build, 0)

    def out_copy(from_plane, group, sender, local=False):
        dest = out.at[:, :, pl.ds(pl.multiple_of((from_plane * CORES + sender) * cols, cols), cols)]
        source = done.at[from_plane, group]
        if local:
            return pltpu.make_async_copy(source, dest, out_send.at[from_plane, group])
        return pltpu.make_async_remote_copy(
            src_ref=source, dst_ref=dest,
            send_sem=out_send.at[from_plane, group], recv_sem=out_recv.at[from_plane, sender],
            **device(plane * CORES + group))

    def multiply(order, from_plane):
        group = jnp.where(low_first, order, CORES - 1 - order)

        def one(r, carry):
            i = group * own_tiles + r
            begin = window_start(first + i, tiles) - first + REACH
            total = None
            for t in range(WIDE):
                right = jnp.concatenate([held[from_plane, c, begin + t] for c in range(2)], axis=0)
                term = jnp.dot(left[i, t], right, preferred_element_type=jnp.float32)
                total = term if total is None else total + term
            rows = pl.ds(pl.multiple_of(r * TILE, TILE), TILE)
            done[from_plane, group, 0, rows, :] = total[:TILE].astype(jnp.bfloat16)
            done[from_plane, group, 1, rows, :] = total[TILE:].astype(jnp.bfloat16)
            return carry

        lax.fori_loop(0, own_tiles, one, 0)

        @pl.when(group == m)
        def _():
            out_copy(from_plane, group, m, local=True).start()

        @pl.when(group != m)
        def _():
            out_copy(from_plane, group, m).start()

    own_columns(lambda copy: copy.wait())

    def own(order, carry):
        multiply(order, plane)
        return carry

    lax.fori_loop(0, CORES, own, 0)

    ready = [steps - 1 if g == CORES - 1 else 2 * g + 4 for g in range(CORES)]
    for step in range(steps):
        if step and step + AHEAD - 1 < steps:
            send_step(step + AHEAD - 1)
        for o in offsets:
            sender = lax.rem(plane + planes - o, planes)
            parts(step, plane, sender, True, lambda copy: copy.wait_recv())
            if step == 0:
                @pl.when(sender // 2 != plane // 2)
                def _():
                    pass_on(sender, start)
            elif step in ready:
                multiply(ready.index(step), sender)

    for u in range(own_tiles):
        for kind in range(3):
            band_copy(kind, m, u, core_mate).wait_send()

    @pl.when(sends_low)
    def _():
        for u in range(REACH):
            edge_copy(0, u, (plane + 1) * CORES + m).wait_send()

    @pl.when(sends_high)
    def _():
        for u in range(REACH):
            edge_copy(1, u, (plane - 1) * CORES + m).wait_send()

    for side, relays in ((0, relays_low), (1, relays_high)):
        @pl.when(relays)
        def _(side=side):
            edge_relay(side, lambda copy: copy.wait_send())

    for k in range(2):
        pass_on(far_planes[k], lambda copy: copy.wait_send())
    for step in range(steps):
        for o in offsets:
            parts(step, lax.rem(plane + o, planes), plane, False, lambda copy: copy.wait_send())

    def finish(index, carry):
        from_plane, group = index // CORES, index % CORES

        @pl.when(group == m)
        def _():
            out_copy(from_plane, group, m, local=True).wait()

        @pl.when(group != m)
        def _():
            out_copy(from_plane, group, m).wait_send()
            out_copy(from_plane, group, group).wait_recv()

        return carry

    lax.fori_loop(0, planes * CORES, finish, 0)


def by_planes(spectra, pattern, counts):
    _, parts, total, cols = spectra.shape
    devices = lax.axis_size("row")
    planes = devices // CORES
    tiles = total // TILE
    own_tiles = cols // TILE
    plane_tiles = CORES * own_tiles
    reach_tiles = plane_tiles + 2 * REACH
    units = reach_tiles // REACH
    weights = (1.0 / counts.astype(jnp.float32)).reshape(tiles, TILE)
    dma = pltpu.SemaphoreType.DMA
    product = pl.pallas_call(
        functools.partial(plane_kernel, planes),
        out_shape=jax.ShapeDtypeStruct((parts, cols, total), jnp.bfloat16),
        in_specs=[
            pl.BlockSpec(memory_space=pl.ANY),
            pl.BlockSpec(memory_space=pltpu.SMEM),
            pl.BlockSpec(memory_space=pltpu.VMEM),
        ],
        out_specs=pl.BlockSpec(memory_space=pl.ANY),
        scratch_shapes=[
            pltpu.VMEM((planes, 2, reach_tiles, TILE, cols), jnp.bfloat16),
            pltpu.VMEM((reach_tiles, 2, WIDE, TILE, TILE), jnp.bfloat16),
            pltpu.VMEM((plane_tiles, WIDE, 2 * TILE, 2 * TILE), jnp.bfloat16),
            pltpu.VMEM((planes, CORES, 2, cols, cols), jnp.bfloat16),
            dma((3, own_tiles)),
            dma((4, own_tiles)),
            dma((2, REACH, CORES)),
            dma((2, REACH)),
            dma((planes, units)),
            dma((planes, units)),
            dma((planes,)),
            dma((planes, CORES)),
            dma((planes, CORES)),
        ],
        compiler_params=pltpu.CompilerParams(
            collective_id=0, has_side_effects=True, vmem_limit_bytes=VMEM_BYTES),
        cost_estimate=pl.CostEstimate(
            flops=4 * total * parts * cols * WIDE * TILE, bytes_accessed=2 * spectra.nbytes, transcendentals=0),
    )(spectra.reshape(parts, tiles, TILE, cols), pattern, weights)
    return product[None]


def fits(spectra):
    devices = lax.axis_size("row")
    cols = spectra.shape[3]
    return devices == 4 * CORES and cols == 2 * REACH * TILE and spectra.shape[0] == 1


def per_device(spectra, pattern, counts):
    if fits(spectra):
        return by_planes(spectra, pattern, counts)
    return by_rows(spectra, pattern, counts)


def solution(mesh):
    return jax.shard_map(
        per_device,
        mesh=mesh,
        in_specs=(P("groups", None, None, "row"), P(), P()),
        out_specs=P("groups", None, "row", None),
        check_vma=False,
    )
```

```python
import functools

import jax
import jax.numpy as jnp
from jax import lax
from jax.experimental import pallas as pl
from jax.experimental.pallas import tpu as pltpu
from jax.sharding import PartitionSpec as P

TILE = 128
REACH = 2
WIDE = 2 * REACH + 1
CORES = 4
AHEAD = 4
VMEM_BYTES = 62 * 2**20


def from_behind(value, axis, steps):
    count = lax.axis_size(axis)
    initial, last = (max(0, -steps), min(count, count - steps))
    return lax.ppermute(value, axis, [(source, source + steps) for source in range(initial, last)])


def by_rows(spectra, pattern, counts):
    total = spectra.shape[2]
    rows_dev = spectra.shape[3]
    place = lax.axis_index("row")
    margin = REACH * TILE
    span = max(rows_dev, TILE) + 2 * margin
    tiles = total // TILE
    first_tile = place * rows_dev // TILE
    offset_rows = place * rows_dev - first_tile * TILE
    own_rows = lax.all_to_all(spectra, "row", split_axis=2, concat_axis=3, tiled=True)
    below = (margin + max(TILE - rows_dev, 0) + rows_dev - 1) // rows_dev
    above = (span - margin + rows_dev - 1) // rows_dev - 1
    pieces = []
    for offset in range(-below, above + 1):
        if offset == 0:
            pieces.append(own_rows)
        else:
            pieces.append(from_behind(own_rows, "row", -offset))
    joined = jnp.concatenate(pieces, axis=2)
    window = lax.dynamic_slice_in_dim(joined, below * rows_dev - margin - offset_rows, span, 2)
    tile_range = jnp.arange(tiles, dtype=jnp.int32)
    row_ids = place * rows_dev + jnp.arange(rows_dev, dtype=jnp.int32)
    inner_ids = (first_tile - REACH) * TILE + jnp.arange(span, dtype=jnp.int32)
    row_onehot = (row_ids[:, None] // TILE == tile_range[None, :]).astype(jnp.float32)
    inner_onehot = (inner_ids[:, None] // TILE == tile_range[None, :]).astype(jnp.float32)
    pattern_rows = jnp.dot(row_onehot, pattern.astype(jnp.float32), precision=lax.Precision.HIGHEST)
    aperture = jnp.dot(pattern_rows, inner_onehot.T, precision=lax.Precision.HIGHEST)
    padded_counts = jnp.pad(counts, (margin, margin), constant_values=1)
    weights = 1.0 / lax.dynamic_slice_in_dim(padded_counts, first_tile * TILE, span).astype(
        jnp.float32
    )
    factor = aperture * weights[None, :]
    wide_rows = jnp.pad(own_rows, ((0, 0), (0, 0), (0, 0), (margin, margin)))
    columns = lax.dynamic_slice_in_dim(wide_rows, first_tile * TILE, span, 3)
    left = (columns[0].astype(jnp.float32) * factor[None]).astype(jnp.bfloat16)
    stacked_left = jnp.concatenate(
        [jnp.concatenate([left[0], -left[1]], axis=1), jnp.concatenate([left[1], left[0]], axis=1)],
        axis=0,
    )
    product = jnp.dot(
        stacked_left, window[0].reshape(2 * span, total), preferred_element_type=jnp.float32
    )
    results = [product.astype(jnp.bfloat16).reshape(2, rows_dev, total)]
    return jnp.stack(results)


def window_start(tile, tiles):
    return jnp.clip(tile - REACH, 0, tiles - WIDE)


def plane_kernel(planes, src, pat, weights, out, held, band, left, done,
                 band_send, band_recv, edge_send, edge_recv,
                 part_send, part_recv, pass_send, out_send, out_recv):
    tiles = src.shape[1]
    cols = src.shape[3]
    own_tiles = cols // TILE
    plane_tiles = CORES * own_tiles
    me = lax.axis_index("row")
    plane = me // CORES
    m = me % CORES
    core_mate = me + 1 - 2 * (me % 2)
    x_mate = plane * CORES + (m + 2) % CORES
    first = plane * plane_tiles
    low_first = m >= 2
    odd = plane % 2
    far_planes = [2 - 2 * (plane // 2) + k for k in range(2)]

    def device(index):
        return dict(device_id={"row": index}, device_id_type=pl.DeviceIdType.MESH)

    barrier = pltpu.get_barrier_semaphore()
    count = planes * CORES

    def greet(step, carry):
        pl.semaphore_signal(barrier, inc=1, **device(lax.rem(me + step, count)))
        return carry

    lax.fori_loop(1, count, greet, 0)
    pl.semaphore_wait(barrier, count - 1)

    def band_view(u):
        tile = me * own_tiles + u
        return src.at[:, pl.ds(window_start(tile, tiles), WIDE), :, pl.ds(u * TILE, TILE)]

    def band_slot(member, u):
        return band.at[member * own_tiles + u + REACH]

    def band_copy(kind, member, u, target):
        source = band_slot(member, u) if kind == 2 else band_view(u)
        return pltpu.make_async_remote_copy(
            src_ref=source, dst_ref=band_slot(member, u),
            send_sem=band_send.at[kind, u], recv_sem=band_recv.at[kind, u], **device(target))

    def band_local(u):
        return pltpu.make_async_copy(band_view(u), band_slot(m, u), band_recv.at[3, u])

    for u in range(own_tiles):
        band_copy(1, m, u, x_mate).start()
    for u in range(own_tiles):
        band_local(u).start()
        band_copy(0, m, u, core_mate).start()

    def edge_copy(side, u, dest, relay=0):
        if side == 0:
            column = own_tiles - REACH + u
            row, slot, place = me * own_tiles + column + 1, u, WIDE - REACH
        else:
            column = u
            row, slot, place = me * own_tiles + column - REACH, plane_tiles + REACH + u, 0
        row = jnp.clip(row, 0, tiles - REACH)
        landing = band.at[slot, :, pl.ds(place, REACH)]
        source = landing if relay else src.at[:, pl.ds(row, REACH), :, pl.ds(column * TILE, TILE)]
        return pltpu.make_async_remote_copy(
            src_ref=source, dst_ref=landing,
            send_sem=edge_send.at[side, u, relay], recv_sem=edge_recv.at[side, u],
            **device(dest))

    sends_low = jnp.logical_and(m == CORES - 1, plane < planes - 1)
    sends_high = jnp.logical_and(m == 0, plane > 0)

    @pl.when(sends_low)
    def _():
        for u in range(REACH):
            edge_copy(0, u, (plane + 1) * CORES + m).start()

    @pl.when(sends_high)
    def _():
        for u in range(REACH):
            edge_copy(1, u, (plane - 1) * CORES + m).start()

    units = plane_tiles // REACH + 2

    def unit_copy(unit, to_plane, from_plane):
        start = unit * REACH
        return pltpu.make_async_remote_copy(
            src_ref=src.at[:, pl.ds(to_plane * plane_tiles - REACH + start, REACH)],
            dst_ref=held.at[from_plane, :, pl.ds(start, REACH)],
            send_sem=part_send.at[to_plane, unit], recv_sem=part_recv.at[from_plane, unit],
            **device(to_plane * CORES + m))

    def parts(step, to_plane, from_plane, receiving, act):
        low_edge = to_plane % 2 == 1
        shared = jnp.where(low_edge, 1, units - 2)
        far = to_plane // 2 != from_plane // 2

        def one_end(unit):
            exists = jnp.where(unit == 0, to_plane > 0, to_plane < planes - 1)
            passed_on = jnp.logical_and(far, jnp.where(low_edge, unit == 0, unit == units - 1))
            if not receiving:
                exists = jnp.logical_and(exists, jnp.logical_not(passed_on))

            @pl.when(exists)
            def _():
                act(unit_copy(unit, to_plane, from_plane))

        if step == 0:
            act(unit_copy(shared, to_plane, from_plane))
        elif step == 1:
            one_end(jnp.where(low_first, 0, units - 1))
        elif step == units - 1:
            one_end(jnp.where(low_first, units - 1, 0))
        else:
            j = step - 2
            act(unit_copy(jnp.where(low_first, jnp.where(low_edge, 2 + j, 1 + j),
                                    jnp.where(low_edge, units - 2 - j, units - 3 - j)),
                          to_plane, from_plane))

    def pass_on(from_plane, act):
        mine = jnp.where(odd == 1, 1, units - 2)
        theirs = jnp.where(odd == 1, units - 1, 0)
        act(pltpu.make_async_remote_copy(
            src_ref=held.at[from_plane, :, pl.ds(mine * REACH, REACH)],
            dst_ref=held.at[from_plane, :, pl.ds(theirs * REACH, REACH)],
            send_sem=pass_send.at[from_plane], recv_sem=part_recv.at[from_plane, theirs],
            **device((plane + 1 - 2 * odd) * CORES + m)))

    def own_columns(act):
        def piece(start, size, k):
            act(pltpu.make_async_copy(
                src.at[:, pl.ds(first - REACH + start, size)],
                held.at[plane, :, pl.ds(start, size)], part_recv.at[plane, k]))

        piece(REACH, plane_tiles, 1)

        @pl.when(plane > 0)
        def _():
            piece(0, REACH, 0)

        @pl.when(plane < planes - 1)
        def _():
            piece(REACH + plane_tiles, REACH, units - 1)

    def start(copy):
        copy.start()

    steps = units
    offsets = [o for k in range(planes // 2, 0, -1) for o in dict.fromkeys((k, planes - k))]

    def send_step(step):
        for o in offsets:
            parts(step, lax.rem(plane + o, planes), plane, False, start)

    own_columns(start)
    for step in range(AHEAD):
        send_step(step)

    for u in range(own_tiles):
        band_copy(1, (m + 2) % CORES, u, x_mate).wait_recv()
        band_copy(2, (m + 2) % CORES, u, core_mate).start()
    core_m = core_mate % CORES
    for u in range(own_tiles):
        band_local(u).wait()
        band_copy(0, core_m, u, core_mate).wait_recv()
        band_copy(2, (core_m + 2) % CORES, u, core_mate).wait_recv()

    relays_low = jnp.logical_and(m == CORES - 1, plane > 0)
    relays_high = jnp.logical_and(m == 0, plane < planes - 1)

    def edge_relay(side, act):
        for u in range(REACH):
            for hop in range(1, CORES):
                act(edge_copy(side, u, plane * CORES + (m + hop) % CORES, hop))

    for side, present, relays in ((0, plane > 0, relays_low), (1, plane < planes - 1, relays_high)):
        @pl.when(present)
        def _(side=side):
            for u in range(REACH):
                edge_copy(side, u, me).wait_recv()

        @pl.when(relays)
        def _(side=side):
            edge_relay(side, lambda copy: copy.start())

    def build(index, carry):
        i, t = index // WIDE, index % WIDE
        tile = first + i
        inner = window_start(tile, tiles) + t
        j = jnp.clip(tile - window_start(inner, tiles), 0, WIDE - 1)
        slot = inner - first + REACH
        factor = pat[tile, inner].astype(jnp.float32) * weights[pl.ds(inner, 1), :]
        re = (band[slot, 0, j].astype(jnp.float32) * factor).astype(jnp.bfloat16)
        im = (band[slot, 1, j].astype(jnp.float32) * factor).astype(jnp.bfloat16)
        left[i, t, 0:TILE, 0:TILE] = re
        left[i, t, 0:TILE, TILE:2 * TILE] = -im
        left[i, t, TILE:2 * TILE, 0:TILE] = im
        left[i, t, TILE:2 * TILE, TILE:2 * TILE] = re
        return carry

    lax.fori_loop(0, plane_tiles * WIDE, build, 0)

    def out_copy(from_plane, group, sender, local=False):
        dest = out.at[:, :, pl.ds(pl.multiple_of((from_plane * CORES + sender) * cols, cols), cols)]
        source = done.at[from_plane, group]
        if local:
            return pltpu.make_async_copy(source, dest, out_send.at[from_plane, group])
        return pltpu.make_async_remote_copy(
            src_ref=source, dst_ref=dest,
            send_sem=out_send.at[from_plane, group], recv_sem=out_recv.at[from_plane, sender],
            **device(plane * CORES + group))

    def multiply(order, from_plane):
        group = jnp.where(low_first, order, CORES - 1 - order)

        def one(r, carry):
            i = group * own_tiles + r
            begin = window_start(first + i, tiles) - first + REACH
            total = None
            for t in range(WIDE):
                right = jnp.concatenate([held[from_plane, c, begin + t] for c in range(2)], axis=0)
                term = jnp.dot(left[i, t], right, preferred_element_type=jnp.float32)
                total = term if total is None else total + term
            rows = pl.ds(pl.multiple_of(r * TILE, TILE), TILE)
            done[from_plane, group, 0, rows, :] = total[:TILE].astype(jnp.bfloat16)
            done[from_plane, group, 1, rows, :] = total[TILE:].astype(jnp.bfloat16)
            return carry

        lax.fori_loop(0, own_tiles, one, 0)

        @pl.when(group == m)
        def _():
            out_copy(from_plane, group, m, local=True).start()

        @pl.when(group != m)
        def _():
            out_copy(from_plane, group, m).start()

    own_columns(lambda copy: copy.wait())

    def own(order, carry):
        multiply(order, plane)
        return carry

    lax.fori_loop(0, CORES, own, 0)

    ready = [steps - 1 if g == CORES - 1 else 2 * g + 4 for g in range(CORES)]
    for step in range(steps):
        if step and step + AHEAD - 1 < steps:
            send_step(step + AHEAD - 1)
        for o in offsets:
            sender = lax.rem(plane + planes - o, planes)
            parts(step, plane, sender, True, lambda copy: copy.wait_recv())
            if step == 0:
                @pl.when(sender // 2 != plane // 2)
                def _():
                    pass_on(sender, start)
            elif step in ready:
                multiply(ready.index(step), sender)

    for u in range(own_tiles):
        for kind in range(3):
            band_copy(kind, m, u, core_mate).wait_send()

    @pl.when(sends_low)
    def _():
        for u in range(REACH):
            edge_copy(0, u, (plane + 1) * CORES + m).wait_send()

    @pl.when(sends_high)
    def _():
        for u in range(REACH):
            edge_copy(1, u, (plane - 1) * CORES + m).wait_send()

    for side, relays in ((0, relays_low), (1, relays_high)):
        @pl.when(relays)
        def _(side=side):
            edge_relay(side, lambda copy: copy.wait_send())

    for k in range(2):
        pass_on(far_planes[k], lambda copy: copy.wait_send())
    for step in range(steps):
        for o in offsets:
            parts(step, lax.rem(plane + o, planes), plane, False, lambda copy: copy.wait_send())

    def finish(index, carry):
        from_plane, group = index // CORES, index % CORES

        @pl.when(group == m)
        def _():
            out_copy(from_plane, group, m, local=True).wait()

        @pl.when(group != m)
        def _():
            out_copy(from_plane, group, m).wait_send()
            out_copy(from_plane, group, group).wait_recv()

        return carry

    lax.fori_loop(0, planes * CORES, finish, 0)


def by_planes(spectra, pattern, counts):
    _, parts, total, cols = spectra.shape
    devices = lax.axis_size("row")
    planes = devices // CORES
    tiles = total // TILE
    own_tiles = cols // TILE
    plane_tiles = CORES * own_tiles
    reach_tiles = plane_tiles + 2 * REACH
    units = reach_tiles // REACH
    weights = (1.0 / counts.astype(jnp.float32)).reshape(tiles, TILE)
    dma = pltpu.SemaphoreType.DMA
    product = pl.pallas_call(
        functools.partial(plane_kernel, planes),
        out_shape=jax.ShapeDtypeStruct((parts, cols, total), jnp.bfloat16),
        in_specs=[
            pl.BlockSpec(memory_space=pl.ANY),
            pl.BlockSpec(memory_space=pltpu.SMEM),
            pl.BlockSpec(memory_space=pltpu.VMEM),
        ],
        out_specs=pl.BlockSpec(memory_space=pl.ANY),
        scratch_shapes=[
            pltpu.VMEM((planes, 2, reach_tiles, TILE, cols), jnp.bfloat16),
            pltpu.VMEM((reach_tiles, 2, WIDE, TILE, TILE), jnp.bfloat16),
            pltpu.VMEM((plane_tiles, WIDE, 2 * TILE, 2 * TILE), jnp.bfloat16),
            pltpu.VMEM((planes, CORES, 2, cols, cols), jnp.bfloat16),
            dma((3, own_tiles)),
            dma((4, own_tiles)),
            dma((2, REACH, CORES)),
            dma((2, REACH)),
            dma((planes, units)),
            dma((planes, units)),
            dma((planes,)),
            dma((planes, CORES)),
            dma((planes, CORES)),
        ],
        compiler_params=pltpu.CompilerParams(
            collective_id=0, has_side_effects=True, vmem_limit_bytes=VMEM_BYTES),
        cost_estimate=pl.CostEstimate(
            flops=4 * total * parts * cols * WIDE * TILE, bytes_accessed=2 * spectra.nbytes, transcendentals=0),
    )(spectra.reshape(parts, tiles, TILE, cols), pattern, weights)
    return product[None]


def fits(spectra):
    devices = lax.axis_size("row")
    cols = spectra.shape[3]
    return devices == 4 * CORES and cols == 2 * REACH * TILE and spectra.shape[0] == 1


def per_device(spectra, pattern, counts):
    if fits(spectra):
        return by_planes(spectra, pattern, counts)
    return by_rows(spectra, pattern, counts)


def solution(mesh):
    return jax.shard_map(
        per_device,
        mesh=mesh,
        in_specs=(P("groups", None, None, "row"), P(), P()),
        out_specs=P("groups", None, "row", None),
        check_vma=False,
    )
```
